512 devices in a mesh: wide: 64 (over y_hi, z, core), narrow: 8 (over x, y_lo).
Axes of the slice: x: 4, y: 8 (y_hi: 4, y_lo: 2; y = y_hi * 2 + y_lo), z: 8, core: 2. Of those that a mesh axis runs over, the one named last changes fastest.
Arguments:
- caption_vectors: bfloat16 [65536, 1152], P(('wide', 'narrow'))
- picture_vectors: bfloat16 [65536, 1152], P(('wide', 'narrow'))
- matching_picture_index: int32 [65536], P(('wide', 'narrow')), may hold values from 0 to 65535, as said below
- sharpness_multiplier: float32 [], replicated, may hold values from 4 to 8
- offset_shift: float32 [], replicated, may hold values from -3 to -1
Outputs:
- text_grad: bfloat16 [65536, 1152], P(('wide', 'narrow'))
- image_grad: bfloat16 [65536, 1152], P(('wide', 'narrow'))
The draws below stay inside these ranges and needn't reach their ends.
Inputs may be any that keep to these rules, and one draw needn't show every extreme that they name: `matching_picture_index`: the text rows k * 128 to (k + 1) * 128 - 1 match the image rows of the same range, one to one.
All inputs are finite; a program needn't handle non-finite values.
Results may differ from the reference program's by a relative error of at most 0.018.
Values may be sent and summed in bfloat16 or wider, within the bound.
No kernel may reach another device: no remote copies, remote signals or barrier semaphores. Data moves between devices by JAX's collectives and lax.ppermute only.
A program may use at most 64 MiB of HBM per device.

```python
import jax
import jax.numpy as jnp
from jax import lax

D = 1152
ROWS = 128
STEPS = 4
GROUP = 1024
PAIRS = 65536
N_NARROW = 8


def scaled_rows(key):
    row_key, col_key, val_key = jax.random.split(key, 3)
    row_scale = 10.0 ** jax.random.uniform(row_key, (PAIRS, 1), jnp.float32, -0.5, 0.5)
    col_scale = 10.0 ** jax.random.uniform(col_key, (1, D), jnp.float32, -0.5, 0.5)
    value_entries = jax.random.normal(val_key, (PAIRS, D), jnp.float32)
    return (value_entries * row_scale * col_scale).astype(jnp.bfloat16)


def draw_caption_vectors(key, part):
    key = jax.random.fold_in(key, 11)
    return scaled_rows(key)


def draw_picture_vectors(key, part):
    key = jax.random.fold_in(key, 23)
    return scaled_rows(key)


def draw_matching_picture_index(key, part):
    key = jax.random.fold_in(key, 37)
    blocks = PAIRS // ROWS
    keys = jax.random.split(key, blocks)
    orders = jax.vmap(lambda single: jax.random.permutation(single, ROWS))(keys).astype(jnp.int32)
    starts = (jnp.arange(blocks, dtype=jnp.int32) * ROWS)[:, None]
    return (orders + starts).reshape(PAIRS).astype(jnp.int32)


def setup_inputs(seed: int = 0) -> dict:
    arg_keys = jax.random.split(jax.random.key(seed), 6)
    caption_vectors = draw_caption_vectors(jax.random.fold_in(arg_keys[5], 71), 0)
    picture_vectors = draw_picture_vectors(jax.random.fold_in(arg_keys[5], 71), 0)
    matching_picture_index = draw_matching_picture_index(jax.random.fold_in(arg_keys[5], 71), 0)
    sharpness_multiplier = jnp.clip(jax.random.uniform(arg_keys[3], (), jnp.float32, 4.0, 8.0), 4.0, 8.0)
    offset_shift = jnp.clip(jax.random.uniform(arg_keys[4], (), jnp.float32, -3.0, -1.0), -3.0, -1.0)
    return dict(caption_vectors=caption_vectors, picture_vectors=picture_vectors, matching_picture_index=matching_picture_index, sharpness_multiplier=sharpness_multiplier, offset_shift=offset_shift)


def normalized_rows(value_entries):
    wide_vals = value_entries.astype(jnp.float32)
    inverse = lax.rsqrt(lax.optimization_barrier(jnp.sum(wide_vals * wide_vals, axis=-1, keepdims=True)) + 1e-06)
    return (wide_vals * inverse).astype(jnp.bfloat16)

def reference(caption_vectors, picture_vectors, matching_picture_index, sharpness_multiplier, offset_shift):
    groups = PAIRS // GROUP
    text_unit = normalized_rows(caption_vectors).reshape(groups, GROUP, D)
    image_unit = normalized_rows(picture_vectors).reshape(groups, GROUP, D)
    label_rows = matching_picture_index.reshape(groups, GROUP)
    offsets = jnp.arange(STEPS, dtype=jnp.int32)
    columns = jnp.arange(GROUP, dtype=jnp.int32)

    def one_group(buffer, group_index):
        picks = ((group_index - offsets) % groups).astype(jnp.int32)
        chosen = jnp.take(text_unit, picks, axis=0)
        chosen_labels = jnp.take(label_rows, picks, axis=0)
        image_tile_rows = image_unit[group_index]
        cosine_agreement = jnp.einsum('sgd,id->sgi', chosen.astype(jnp.float32), image_tile_rows.astype(jnp.float32))
        couple_odds_table = sharpness_multiplier * cosine_agreement + offset_shift
        matched = chosen_labels[:, :, None] == (group_index * GROUP + columns)[None, None, :]
        couple_target_polarity = jnp.where(matched, 1.0, -1.0).astype(jnp.float32)
        objective_weight = (-couple_target_polarity * sharpness_multiplier * jax.nn.sigmoid(-couple_target_polarity * couple_odds_table)).astype(jnp.bfloat16)
        coef_blocks = objective_weight.reshape(STEPS, N_NARROW, ROWS, GROUP).astype(jnp.float32)
        text_blocks = chosen.reshape(STEPS, N_NARROW, ROWS, D).astype(jnp.float32)
        partial_value = jnp.einsum('snri,snrd->nid', coef_blocks, text_blocks).astype(jnp.bfloat16)
        image_portion = lax.optimization_barrier(jnp.sum(partial_value.astype(jnp.float32), axis=0)).astype(jnp.bfloat16)
        pieces = jnp.einsum('sgi,id->sgd', objective_weight.astype(jnp.float32), image_tile_rows.astype(jnp.float32))
        buffer = buffer.at[picks].add(pieces)
        return (buffer, image_portion)
    start = jnp.zeros((groups, GROUP, D), jnp.float32)
    buffer, image_parts = lax.scan(one_group, start, jnp.arange(groups, dtype=jnp.int32))
    text_grad = buffer.reshape(PAIRS, D).astype(jnp.bfloat16)
    image_grad = image_parts.reshape(PAIRS, D)
    return (text_grad, image_grad)
```

```python
import functools

import jax
import jax.numpy as jnp
from jax import lax
from jax.experimental import pallas as pl
from jax.experimental.pallas import tpu as pltpu
from jax.sharding import PartitionSpec as P

STEPS = 4
PIECES = 2
TILE = 256


def normalized_rows(value_entries):
    wide_vals = value_entries.astype(jnp.float32)
    inverse = lax.rsqrt(jnp.sum(wide_vals * wide_vals, axis=-1, keepdims=True) + 1e-06)
    return (wide_vals * inverse).astype(jnp.bfloat16)


def unit_kernel(text_ref, image_ref, text_out, *image_outs):
    rows = image_outs[0].shape[1]
    for piece, out in enumerate(image_outs):
        unit = normalized_rows(image_ref[piece * rows : (piece + 1) * rows, :])
        for receiver in range(out.shape[0]):
            out[receiver] = unit
    text_out[...] = normalized_rows(text_ref[...])


def unit_call(text, image, receivers):
    rows, width = text.shape
    piece = rows // PIECES
    shapes = [jax.ShapeDtypeStruct(text.shape, jnp.bfloat16)]
    shapes += [jax.ShapeDtypeStruct((receivers, piece, width), jnp.bfloat16)] * PIECES
    return pl.pallas_call(
        unit_kernel,
        out_shape=shapes,
        compiler_params=pltpu.CompilerParams(vmem_limit_bytes=32 * 1024 * 1024),
    )(text, image)


def pair_kernel(piece, rows, scalars_ref, place_ref, label_ref, text_ref, image_ref, *rest):
    if piece:
        start_ref, partial_ref, sum_ref = rest
    else:
        partial_ref, sum_ref = rest
    tile = pl.program_id(0)
    scale, shift = scalars_ref[0], scalars_ref[1]
    text, image = text_ref[...], image_ref[...]
    score = lax.dot_general(
        text, image, (((1,), (1,)), ((), ())), preferred_element_type=jnp.float32
    )
    chance = 1.0 / (1.0 + jnp.exp(-(scale * score + shift)))
    own = rows
    part = rows // PIECES
    column = tile * TILE + lax.broadcasted_iota(jnp.int32, (own, TILE), 1)
    image_row = (column // part) * rows + piece * part + column % part + place_ref[0]
    matched = label_ref[...] == image_row
    first = chance[:own] - jnp.where(matched, 1.0, 0.0)
    coef = (scale * jnp.concatenate([first, chance[own:]], axis=0)).astype(jnp.bfloat16)
    partial_ref[...] = lax.dot_general(
        coef, text, (((0,), (0,)), ((), ())), preferred_element_type=jnp.float32
    ).astype(jnp.bfloat16)
    grad = jnp.dot(coef, image, preferred_element_type=jnp.float32)

    @pl.when(tile == 0)
    def _():
        sum_ref[...] = (start_ref[...] + grad) if piece else grad

    @pl.when(tile > 0)
    def _():
        sum_ref[...] += grad


def pair_call(piece, scalars, place, labels, texts, images, start):
    count, width = texts.shape
    rows = labels.shape[0]
    whole = lambda shape: pl.BlockSpec(shape, lambda i: (0, 0))
    smem = pl.BlockSpec(memory_space=pltpu.SMEM)
    specs = [smem, smem, whole(labels.shape), whole(texts.shape),
             pl.BlockSpec((TILE, width), lambda i: (i, 0))]
    operands = [scalars, place, labels, texts, images]
    if piece:
        specs.append(whole(start.shape))
        operands.append(start)
    return pl.pallas_call(
        functools.partial(pair_kernel, piece, rows),
        grid=(images.shape[0] // TILE,),
        in_specs=specs,
        out_specs=[pl.BlockSpec((TILE, width), lambda i: (i, 0)), whole(texts.shape)],
        out_shape=[
            jax.ShapeDtypeStruct(images.shape, jnp.bfloat16),
            jax.ShapeDtypeStruct(texts.shape, jnp.float32),
        ],
        compiler_params=pltpu.CompilerParams(vmem_limit_bytes=48 * 1024 * 1024),
    )(*operands)


def local(
    caption_vectors, picture_vectors, matching_picture_index, sharpness_multiplier, offset_shift
):
    rows, width = caption_vectors.shape
    wide, narrow = lax.axis_size("wide"), lax.axis_size("narrow")

    def moved(value, even, odd):
        pairs = [(w, (w + (odd if w % 2 else even)) % wide) for w in range(wide)]
        return lax.ppermute(value, "wide", pairs)

    twins = [[w, w + 1] for w in range(0, wide, 2)]
    text_unit, *image_units = unit_call(caption_vectors, picture_vectors, narrow)
    two_behind = moved(text_unit, 2, 2)
    crossing = moved(text_unit, 1, 3)
    both = lax.all_gather(two_behind, "wide", axis=0, tiled=True, axis_index_groups=twins)
    texts = jnp.concatenate([text_unit, both, crossing], axis=0)
    scalars = jnp.stack([sharpness_multiplier, offset_shift])
    place = (lax.axis_index("wide") * (rows * narrow))[None].astype(jnp.int32)
    labels = matching_picture_index[:, None]
    total, pieces = None, []
    for piece, unit in enumerate(image_units):
        images = lax.all_to_all(
            unit.reshape(-1, width), "narrow", split_axis=0, concat_axis=0, tiled=True
        )
        partial_value, total = pair_call(piece, scalars, place, labels, texts, images, total)
        back = lax.all_to_all(
            partial_value, "narrow", split_axis=0, concat_axis=0, tiled=True
        )
        pieces.append(
            jnp.sum(back.reshape(narrow, -1, width).astype(jnp.float32), axis=0).astype(jnp.bfloat16)
        )
    image_grad = jnp.concatenate(pieces, axis=0)
    swapped = lax.all_to_all(
        total[rows : 3 * rows].astype(jnp.bfloat16), "wide",
        split_axis=0, concat_axis=0, tiled=True, axis_index_groups=twins,
    ).astype(jnp.float32)
    from_two = moved((swapped[:rows] + swapped[rows:]).astype(jnp.bfloat16), -2, -2)
    from_cross_pairs = [(w, (w - (1 if w % 2 else 3)) % wide) for w in range(wide)]
    from_cross = lax.ppermute(total[3 * rows :].astype(jnp.bfloat16), "wide", from_cross_pairs)
    text_grad = total[:rows] + from_two.astype(jnp.float32) + from_cross.astype(jnp.float32)
    return (text_grad.astype(jnp.bfloat16), image_grad)


def solution(mesh):
    placed = (
        P(("wide", "narrow"), None),
        P(("wide", "narrow"), None),
        P(("wide", "narrow")),
        P(),
        P(),
    )
    return jax.shard_map(
        local,
        mesh=mesh,
        in_specs=placed,
        out_specs=(P(("wide", "narrow"), None), P(("wide", "narrow"), None)),
        check_vma=False,
    )
```

```python
import functools

import jax
import jax.numpy as jnp
from jax import lax
from jax.experimental import pallas as pl
from jax.experimental.pallas import tpu as pltpu
from jax.sharding import PartitionSpec as P

STEPS = 4
TILE = 256


def normalized_rows(value_entries):
    wide_vals = value_entries.astype(jnp.float32)
    inverse = lax.rsqrt(jnp.sum(wide_vals * wide_vals, axis=-1, keepdims=True) + 1e-06)
    return (wide_vals * inverse).astype(jnp.bfloat16)


def pair_kernel(last, scalars_ref, place_ref, label_ref, *refs):
    text_refs, image_ref, refs = refs[:STEPS], refs[STEPS], refs[STEPS + 1 :]
    if last:
        start_ref, partial_ref, own_ref, mine_ref, other_ref, cross_ref, text = refs
    else:
        partial_ref, sum_ref, text = refs
    scale, shift = scalars_ref[0], scalars_ref[1]
    rows = text_refs[0].shape[0]
    for i, ref in enumerate(text_refs):
        text[i * rows : (i + 1) * rows, :] = normalized_rows(ref[...])
    grad = start_ref[...] if last else None
    for tile in range(image_ref.shape[0] // TILE):
        image = normalized_rows(image_ref[tile * TILE : (tile + 1) * TILE, :])
        score = lax.dot_general(
            text[...], image, (((1,), (1,)), ((), ())), preferred_element_type=jnp.float32
        )
        chance = 1.0 / (1.0 + jnp.exp(-(scale * score + shift)))
        column = tile * TILE + lax.broadcasted_iota(jnp.int32, (rows, TILE), 1)
        image_row = (column // rows) * (2 * rows) + column % rows + place_ref[0]
        matched = label_ref[...] == image_row
        first = chance[:rows] - jnp.where(matched, 1.0, 0.0)
        coef = (scale * jnp.concatenate([first, chance[rows:]], axis=0)).astype(jnp.bfloat16)
        partial_ref[tile * TILE : (tile + 1) * TILE, :] = lax.dot_general(
            coef, text[...], (((0,), (0,)), ((), ())), preferred_element_type=jnp.float32
        ).astype(jnp.bfloat16)
        more = jnp.dot(coef, image, preferred_element_type=jnp.float32)
        grad = more if grad is None else grad + more
    if last:
        own_ref[...] = grad[:rows]
        mine_ref[...] = grad[rows : 2 * rows]
        other_ref[...] = grad[2 * rows : 3 * rows].astype(jnp.bfloat16)
        cross_ref[...] = grad[3 * rows :].astype(jnp.bfloat16)
    else:
        sum_ref[...] = grad


def pair_call(scalars, place, labels, texts, images, start):
    rows, width = texts[0].shape
    last = start is not None
    smem = pl.BlockSpec(memory_space=pltpu.SMEM)
    vmem = pl.BlockSpec(memory_space=pltpu.VMEM)
    one = (rows, width)
    shapes = [jax.ShapeDtypeStruct(images.shape, jnp.bfloat16)]
    if last:
        shapes += [jax.ShapeDtypeStruct(one, t) for t in (jnp.float32, jnp.float32, jnp.bfloat16, jnp.bfloat16)]
    else:
        shapes += [jax.ShapeDtypeStruct((STEPS * rows, width), jnp.float32)]
    operands = [scalars, place, labels, *texts, images] + ([start] if last else [])
    return pl.pallas_call(
        functools.partial(pair_kernel, last),
        in_specs=[smem, smem] + [vmem] * (len(operands) - 2),
        out_specs=[vmem] * len(shapes),
        out_shape=shapes,
        scratch_shapes=[pltpu.VMEM((STEPS * rows, width), jnp.bfloat16)],
        compiler_params=pltpu.CompilerParams(vmem_limit_bytes=48 * 1024 * 1024),
    )(*operands)


def local(
    caption_vectors, picture_vectors, matching_picture_index, sharpness_multiplier, offset_shift
):
    rows, width = caption_vectors.shape
    wide, narrow = lax.axis_size("wide"), lax.axis_size("narrow")
    over_x = [[2 * x + y for x in range(narrow // 2)] for y in range(2)]

    def along_wide(value, even, odd):
        pairs = [(w, (w + (odd if w % 2 else even)) % wide) for w in range(wide)]
        return lax.ppermute(value, "wide", pairs)

    def twin(value):
        return along_wide(value, 1, -1)

    def across(value):
        return lax.ppermute(value, "narrow", [(n, n ^ 1) for n in range(narrow)])

    def exchange(value):
        return lax.all_to_all(
            value, "narrow", split_axis=0, concat_axis=0, tiled=True, axis_index_groups=over_x
        )

    def spread(value):
        return exchange(jnp.concatenate([value] * (narrow // 2), axis=0))

    def gathered_sum(value):
        return jnp.sum(exchange(value).reshape(-1, rows, width).astype(jnp.float32), axis=0)

    swapped = across(picture_vectors)
    mine = along_wide(caption_vectors, 2, 2)
    cross = along_wide(caption_vectors, 1, 3)
    near = spread(picture_vectors)
    far = spread(swapped)
    texts = [caption_vectors, mine, twin(mine), cross]

    scalars = jnp.stack([sharpness_multiplier, offset_shift])
    side = lax.axis_index("narrow") % 2
    start_row = lax.axis_index("wide") * (rows * narrow) + jnp.stack([1 - side, side]) * rows
    start_row = start_row.astype(jnp.int32)
    labels = matching_picture_index[:, None]
    far_partial, total = pair_call(scalars, start_row[:1], labels, texts, far, None)
    far_sum = across(gathered_sum(far_partial).astype(jnp.bfloat16))
    near_partial, own, kept, other, crossed = pair_call(
        scalars, start_row[1:], labels, texts, near, total
    )
    image_grad = gathered_sum(near_partial) + far_sum.astype(jnp.float32)
    kept = along_wide((kept + twin(other).astype(jnp.float32)).astype(jnp.bfloat16), -2, -2)
    crossed = along_wide(crossed, -3, -1)
    text_grad = own + kept.astype(jnp.float32) + crossed.astype(jnp.float32)
    return (text_grad.astype(jnp.bfloat16), image_grad.astype(jnp.bfloat16))


def solution(mesh):
    placed = (
        P(("wide", "narrow"), None),
        P(("wide", "narrow"), None),
        P(("wide", "narrow")),
        P(),
        P(),
    )
    return jax.shard_map(
        local,
        mesh=mesh,
        in_specs=placed,
        out_specs=(P(("wide", "narrow"), None), P(("wide", "narrow"), None)),
        check_vma=False,
    )
```

```python
import functools

import jax
import jax.numpy as jnp
from jax import lax
from jax.experimental import pallas as pl
from jax.experimental.pallas import tpu as pltpu
from jax.sharding import PartitionSpec as P

STEPS = 4
SIDES = 2
SMEM = pl.BlockSpec(memory_space=pltpu.SMEM)
VMEM = pl.BlockSpec(memory_space=pltpu.VMEM)
ANY = pl.BlockSpec(memory_space=pl.ANY)
HBM = pl.BlockSpec(memory_space=pltpu.HBM)


def params(mebibytes):
    return pltpu.CompilerParams(vmem_limit_bytes=mebibytes * 1024 * 1024)


def normalized_rows(value_entries):
    wide_vals = value_entries.astype(jnp.float32)
    inverse = lax.rsqrt(jnp.sum(wide_vals * wide_vals, axis=-1, keepdims=True) + 1e-06)
    return (wide_vals * inverse).astype(jnp.bfloat16)


def copies_kernel(value_ref, out_ref, sent):
    stores = [
        pltpu.make_async_copy(value_ref, out_ref.at[i], sent.at[i])
        for i in range(out_ref.shape[0])
    ]
    for store in stores:
        store.start()
    for store in stores:
        store.wait()


def copies_call(value, receivers):
    return pl.pallas_call(
        copies_kernel,
        in_specs=[VMEM],
        out_specs=HBM,
        out_shape=pltpu.HBM((receivers, *value.shape), value.dtype),
        scratch_shapes=[pltpu.SemaphoreType.DMA((receivers,))],
        compiler_params=params(8),
    )(value)


def text_kernel(*refs):
    *text_refs, unit_ref = refs
    rows = text_refs[0].shape[0]
    for i, ref in enumerate(text_refs):
        unit_ref[i * rows : (i + 1) * rows, :] = normalized_rows(ref[...])


def text_call(texts, later):
    rows, width = texts[0].shape
    return pl.pallas_call(
        text_kernel,
        in_specs=[VMEM] * len(texts),
        out_specs=VMEM,
        out_shape=jax.ShapeDtypeStruct((len(texts) * rows, width), jnp.bfloat16),
        cost_estimate=pl.CostEstimate(flops=later, bytes_accessed=10**6, transcendentals=0),
        compiler_params=params(8),
    )(*texts)


def chances(scale, shift, text, image):
    score = lax.dot_general(
        image[...], text[...], (((1,), (1,)), ((), ())), preferred_element_type=jnp.float32
    )
    return 1.0 / (1.0 + jnp.exp(-(scale * score + shift)))


def send_partial(coef, text, held, out_ref, sems):
    rows = held.shape[1]
    stores = []
    for i in range(held.shape[0]):
        block = jnp.dot(
            coef[i * rows : (i + 1) * rows, :], text[...], preferred_element_type=jnp.float32
        )
        held[i] = block.astype(jnp.bfloat16)
        store = pltpu.make_async_copy(held.at[i], out_ref.at[i], sems.at[i])
        store.start()
        stores.append(store)
    return stores


def far_kernel(
    scale_ref, shift_ref, near_ref, moved_ref, image_ref, partial_ref, coef_ref,
    text, image, sent, stored,
):
    half = near_ref.shape[0]
    text[:half, :] = near_ref[...]
    text[half:, :] = moved_ref[...]
    image[...] = normalized_rows(image_ref[...])
    scale = scale_ref[0]
    coef = (scale * chances(scale, shift_ref[0], text, image)).astype(jnp.bfloat16)
    coef_ref[...] = coef
    for store in send_partial(coef, text, sent, partial_ref, stored):
        store.wait()


def near_kernel(
    scale_ref, shift_ref, place_ref, label_ref, near_ref, moved_ref, image_ref, far_ref,
    far_coef_ref, partial_ref, own_ref, crossed_ref, kept_ref, other_ref,
    text, image, far, sent, grads, halves, stored, grad_stored,
):
    half = near_ref.shape[0]
    rows = half // 2
    text[:half, :] = near_ref[...]
    text[half:, :] = moved_ref[...]
    image[...] = normalized_rows(image_ref[...])
    scale = scale_ref[0]
    chance = chances(scale, shift_ref[0], text, image)
    far[...] = normalized_rows(far_ref[...])
    index = lax.broadcasted_iota(jnp.int32, (image.shape[0], rows), 0)
    image_row = (index // rows) * (SIDES * rows) + index % rows + place_ref[0]
    matched = jnp.where(label_ref[...] == image_row, 1.0, 0.0)
    chance = jnp.concatenate([chance[:, :rows] - matched, chance[:, rows:]], axis=1)
    coef = (scale * chance).astype(jnp.bfloat16)
    over_images = (((0,), (0,)), ((), ()))
    grad = lax.dot_general(coef, image[...], over_images, preferred_element_type=jnp.float32)
    grad += lax.dot_general(
        far_coef_ref[...], far[...], over_images, preferred_element_type=jnp.float32
    )
    stores = []
    for i, ref in enumerate((own_ref, crossed_ref, kept_ref, other_ref)):
        place = (halves if ref.dtype == jnp.bfloat16 else grads).at[i // 2]
        place[...] = grad[i * rows : (i + 1) * rows].astype(ref.dtype)
        store = pltpu.make_async_copy(place, ref, grad_stored.at[i])
        store.start()
        stores.append(store)
    stores += send_partial(coef, text, sent, partial_ref, stored)
    for store in stores:
        store.wait()


def far_call(scale, shift, texts, far):
    count, width = far.shape
    rows = texts[0].shape[0] // 2
    blocks = (count // rows, rows, width)
    return pl.pallas_call(
        far_kernel,
        in_specs=[SMEM] * 2 + [VMEM] * 3,
        out_specs=[HBM, VMEM],
        out_shape=[
            pltpu.HBM(blocks, jnp.bfloat16),
            jax.ShapeDtypeStruct((count, STEPS * rows), jnp.bfloat16),
        ],
        scratch_shapes=[
            pltpu.VMEM((STEPS * rows, width), jnp.bfloat16),
            pltpu.VMEM((count, width), jnp.bfloat16),
            pltpu.VMEM(blocks, jnp.bfloat16),
            pltpu.SemaphoreType.DMA((blocks[0],)),
        ],
        compiler_params=params(20),
    )(scale, shift, *texts, far)


def near_call(scale, shift, place, labels, texts, near, far, far_coef):
    count, width = near.shape
    rows = texts[0].shape[0] // 2
    blocks = (count // rows, rows, width)
    types = (jnp.float32, jnp.bfloat16, jnp.float32, jnp.bfloat16)
    return pl.pallas_call(
        near_kernel,
        in_specs=[SMEM] * 3 + [VMEM] * 6,
        out_specs=[HBM] * 5,
        out_shape=[pltpu.HBM(blocks, jnp.bfloat16)]
        + [pltpu.HBM((rows, width), kind) for kind in types],
        scratch_shapes=[
            pltpu.VMEM((STEPS * rows, width), jnp.bfloat16),
            pltpu.VMEM((count, width), jnp.bfloat16),
            pltpu.VMEM((count, width), jnp.bfloat16),
            pltpu.VMEM(blocks, jnp.bfloat16),
            pltpu.VMEM((2, rows, width), jnp.float32),
            pltpu.VMEM((2, rows, width), jnp.bfloat16),
            pltpu.SemaphoreType.DMA((blocks[0],)),
            pltpu.SemaphoreType.DMA((len(types),)),
        ],
        compiler_params=params(28),
    )(scale, shift, place, labels, *texts, near, far, far_coef)


def local(
    caption_vectors, picture_vectors, matching_picture_index, sharpness_multiplier, offset_shift
):
    rows, width = caption_vectors.shape
    wide, narrow = lax.axis_size("wide"), lax.axis_size("narrow")
    over_x = [[SIDES * x + y for x in range(narrow // SIDES)] for y in range(SIDES)]

    def along_wide(value, even, odd):
        pairs = [(w, (w + (odd if w % 2 else even)) % wide) for w in range(wide)]
        return lax.ppermute(value, "wide", pairs)

    def twin(value):
        return along_wide(value, 1, -1)

    def across(value):
        return lax.ppermute(value, "narrow", [(n, n ^ 1) for n in range(narrow)])

    def exchange(value):
        return lax.all_to_all(
            value, "narrow", split_axis=0, concat_axis=0, tiled=True, axis_index_groups=over_x
        )

    def spread(value):
        return exchange(copies_call(value, narrow // SIDES)).reshape(-1, width)

    def gathered_sum(value):
        return jnp.sum(exchange(value).astype(jnp.float32), axis=0)

    swapped = across(picture_vectors)
    cross = along_wide(caption_vectors, 1, 3)
    mine = along_wide(caption_vectors, 2, 2)
    near = spread(picture_vectors)
    swapped, near = lax.optimization_barrier((swapped, near))
    far = spread(swapped)
    texts = [text_call([caption_vectors, cross], 6000000000), text_call([mine, twin(mine)], 1000000000)]

    scale, shift = sharpness_multiplier[None], offset_shift[None]
    place = lax.axis_index("wide") * (rows * narrow) + (lax.axis_index("narrow") % SIDES) * rows
    place = place.astype(jnp.int32)[None]
    far_partial, far_coef = far_call(scale, shift, texts, far)
    far_sum = across(gathered_sum(far_partial).astype(jnp.bfloat16))
    near_partial, own, crossed, kept, other = near_call(
        scale, shift, place, matching_picture_index[None, :], texts, near, far, far_coef
    )
    image_grad = gathered_sum(near_partial) + far_sum.astype(jnp.float32)
    kept = along_wide((kept + twin(other).astype(jnp.float32)).astype(jnp.bfloat16), -2, -2)
    crossed = along_wide(crossed, -3, -1)
    text_grad = own + kept.astype(jnp.float32) + crossed.astype(jnp.float32)
    return (text_grad.astype(jnp.bfloat16), image_grad.astype(jnp.bfloat16))


def solution(mesh):
    placed = (
        P(("wide", "narrow"), None),
        P(("wide", "narrow"), None),
        P(("wide", "narrow")),
        P(),
        P(),
    )
    return jax.shard_map(
        local,
        mesh=mesh,
        in_specs=placed,
        out_specs=(P(("wide", "narrow"), None), P(("wide", "narrow"), None)),
        check_vma=False,
    )
```

```python
import functools

import jax
import jax.numpy as jnp
from jax import lax
from jax.experimental import pallas as pl
from jax.experimental.pallas import tpu as pltpu
from jax.sharding import PartitionSpec as P

STEPS = 4
SIDES = 2
PLACES = 16
SMEM = pl.BlockSpec(memory_space=pltpu.SMEM)
VMEM = pl.BlockSpec(memory_space=pltpu.VMEM)
ANY = pl.BlockSpec(memory_space=pl.ANY)
HBM = pl.BlockSpec(memory_space=pltpu.HBM)


def params(mebibytes):
    return pltpu.CompilerParams(vmem_limit_bytes=mebibytes * 1024 * 1024)


def normalized_rows(value_entries):
    wide_vals = value_entries.astype(jnp.float32)
    inverse = lax.rsqrt(jnp.sum(wide_vals * wide_vals, axis=-1, keepdims=True) + 1e-06)
    return (wide_vals * inverse).astype(jnp.bfloat16)


def copies_kernel(value_ref, out_ref, sent):
    stores = [
        pltpu.make_async_copy(value_ref, out_ref.at[i], sent.at[i])
        for i in range(out_ref.shape[0])
    ]
    for store in stores:
        store.start()
    for store in stores:
        store.wait()


def copies_call(value, receivers):
    return pl.pallas_call(
        copies_kernel,
        in_specs=[VMEM],
        out_specs=HBM,
        out_shape=pltpu.HBM((receivers, *value.shape), value.dtype),
        scratch_shapes=[pltpu.SemaphoreType.DMA((receivers,))],
        compiler_params=params(8),
    )(value)


def text_kernel(*refs):
    *text_refs, unit_ref = refs
    rows = text_refs[0].shape[0]
    for i, ref in enumerate(text_refs):
        unit_ref[i * rows : (i + 1) * rows, :] = normalized_rows(ref[...])


def text_call(texts, later):
    rows, width = texts[0].shape
    return pl.pallas_call(
        text_kernel,
        in_specs=[VMEM] * len(texts),
        out_specs=VMEM,
        out_shape=jax.ShapeDtypeStruct((len(texts) * rows, width), jnp.bfloat16),
        cost_estimate=pl.CostEstimate(flops=later, bytes_accessed=10**6, transcendentals=0),
        compiler_params=params(8),
    )(*texts)


def sum_kernel(*refs):
    *value_refs, out_ref = refs
    total = value_refs[0][...].astype(jnp.float32)
    for ref in value_refs[1:]:
        total += ref[...].astype(jnp.float32)
    out_ref[...] = total.astype(out_ref.dtype)


def sum_call(values, kind, later):
    return pl.pallas_call(
        sum_kernel,
        in_specs=[VMEM] * len(values),
        out_specs=VMEM,
        out_shape=jax.ShapeDtypeStruct(values[0].shape, kind),
        cost_estimate=pl.CostEstimate(flops=later, bytes_accessed=10**6, transcendentals=0),
        compiler_params=params(8),
    )(*values)


def join_texts(near_ref, moved_ref, text):
    rows = near_ref.shape[0] // 2
    text[:rows, :] = near_ref[:rows, :]
    text[rows : 2 * rows, :] = near_ref[rows:, :] + moved_ref[2 * rows :, :]
    text[2 * rows :, :] = moved_ref[: 2 * rows, :]


def chances(scale, shift, text, image):
    score = lax.dot_general(
        image[...], text[...], (((1,), (1,)), ((), ())), preferred_element_type=jnp.float32
    )
    return 1.0 / (1.0 + jnp.exp(-(scale * score + shift)))


def send_partial(coef, text, held, out_ref, sems, side):
    rows = held.shape[2]
    stores = []
    for i in range(held.shape[0]):
        block = jnp.dot(
            coef[i * rows : (i + 1) * rows, :], text[...], preferred_element_type=jnp.float32
        )
        held[i, side] = block.astype(jnp.bfloat16)
        store = pltpu.make_async_copy(held.at[i, side], out_ref.at[i, side], sems.at[i, side])
        store.start()
        stores.append(store)
    return stores


def pair_kernel(
    scale_ref, shift_ref, place_ref, label_ref, near_ref, moved_ref, near_image_ref, far_image_ref,
    partial_ref, own_ref, crossed_ref, kept_ref, other_ref,
    text, near, far, sent, grads, halves, stored, grad_stored,
):
    rows = near_ref.shape[0] // 2
    join_texts(near_ref, moved_ref, text)
    near[...] = normalized_rows(near_image_ref[...])
    scale, shift = scale_ref[0], shift_ref[0]
    chance = chances(scale, shift, text, near)
    far[...] = normalized_rows(far_image_ref[...])
    index = lax.broadcasted_iota(jnp.int32, (near.shape[0], rows), 0)
    image_row = (index // rows) * (SIDES * rows) + index % rows + place_ref[0]
    matched = jnp.where(label_ref[...] == image_row, 1.0, 0.0)
    chance = jnp.concatenate([chance[:, :rows] - matched, chance[:, rows:]], axis=1)
    near_coef = (scale * chance).astype(jnp.bfloat16)
    far_coef = (scale * chances(scale, shift, text, far)).astype(jnp.bfloat16)
    stores = send_partial(near_coef, text, sent, partial_ref, stored, 0)
    stores += send_partial(far_coef, text, sent, partial_ref, stored, 1)
    over_images = (((0,), (0,)), ((), ()))
    grad = lax.dot_general(near_coef, near[...], over_images, preferred_element_type=jnp.float32)
    grad += lax.dot_general(far_coef, far[...], over_images, preferred_element_type=jnp.float32)
    for i, ref in enumerate((own_ref, crossed_ref, kept_ref, other_ref)):
        place = (halves if ref.dtype == jnp.bfloat16 else grads).at[i // 2]
        place[...] = grad[i * rows : (i + 1) * rows].astype(ref.dtype)
        store = pltpu.make_async_copy(place, ref, grad_stored.at[i])
        store.start()
        stores.append(store)
    for store in stores:
        store.wait()


def pair_call(scale, shift, place, labels, texts, near, far):
    count, width = near.shape
    rows = texts[0].shape[0] // 2
    blocks = (count // rows, SIDES, rows, width)
    types = (jnp.float32, jnp.bfloat16, jnp.float32, jnp.bfloat16)
    return pl.pallas_call(
        pair_kernel,
        in_specs=[SMEM] * 3 + [VMEM] * 5,
        out_specs=[HBM] * 5,
        out_shape=[pltpu.HBM(blocks, jnp.bfloat16)]
        + [pltpu.HBM((rows, width), kind) for kind in types],
        scratch_shapes=[
            pltpu.VMEM((STEPS * rows, width), jnp.bfloat16),
            pltpu.VMEM((count, width), jnp.bfloat16),
            pltpu.VMEM((count, width), jnp.bfloat16),
            pltpu.VMEM(blocks, jnp.bfloat16),
            pltpu.VMEM((2, rows, width), jnp.float32),
            pltpu.VMEM((2, rows, width), jnp.bfloat16),
            pltpu.SemaphoreType.DMA(blocks[:2]),
            pltpu.SemaphoreType.DMA((len(types),)),
        ],
        compiler_params=params(32),
    )(scale, shift, place, labels, *texts, near, far)


def local(
    caption_vectors, picture_vectors, matching_picture_index, sharpness_multiplier, offset_shift
):
    rows, width = caption_vectors.shape
    wide, narrow = lax.axis_size("wide"), lax.axis_size("narrow")
    over_x = [[SIDES * x + y for x in range(narrow // SIDES)] for y in range(SIDES)]

    def along_wide(value, even, odd, sends=lambda w: True):
        pairs = [(w, (w + (odd if w % 2 else even)) % wide) for w in range(wide) if sends(w)]
        return lax.ppermute(value, "wide", pairs)

    def last(w):
        return w % PLACES >= PLACES - 2

    def first(w):
        return w % PLACES < 2

    def twin(value):
        return along_wide(value, 1, -1)

    def across(value):
        return lax.ppermute(value, "narrow", [(n, n ^ 1) for n in range(narrow)])

    def exchange(value):
        return lax.all_to_all(
            value, "narrow", split_axis=0, concat_axis=0, tiled=True, axis_index_groups=over_x
        )

    def spread(value):
        return exchange(copies_call(value, narrow // SIDES)).reshape(-1, width)

    swapped = across(picture_vectors)
    mine = along_wide(caption_vectors, 2, 2)
    cross = along_wide(caption_vectors, 1, 3, lambda w: w % 2 == 0 or not last(w))
    passed = along_wide(mine, 1, 1, lambda w: w % 2 and first(w))
    near = spread(picture_vectors)
    swapped, near = lax.optimization_barrier((swapped, near))
    far = spread(swapped)
    texts = [text_call([caption_vectors, cross], 6000000000), text_call([mine, twin(mine), passed], 2000000000)]

    scale, shift = sharpness_multiplier[None], offset_shift[None]
    place = lax.axis_index("wide") * (rows * narrow) + (lax.axis_index("narrow") % SIDES) * rows
    place = place.astype(jnp.int32)[None]
    partial_value, own, crossed, kept, other = pair_call(
        scale, shift, place, matching_picture_index[None, :], texts, near, far
    )
    sums = jnp.sum(exchange(partial_value).astype(jnp.float32), axis=0)
    image_grad = sums[0] + across(sums[1].astype(jnp.bfloat16)).astype(jnp.float32)
    kept = along_wide((kept + twin(other).astype(jnp.float32)).astype(jnp.bfloat16), -2, -2)
    crossed = along_wide(crossed, -3, -1)
    text_grad = sum_call([own, kept, crossed], jnp.bfloat16, 10000000)
    return (text_grad, image_grad.astype(jnp.bfloat16))


def solution(mesh):
    placed = (
        P(("wide", "narrow"), None),
        P(("wide", "narrow"), None),
        P(("wide", "narrow")),
        P(),
        P(),
    )
    return jax.shard_map(
        local,
        mesh=mesh,
        in_specs=placed,
        out_specs=(P(("wide", "narrow"), None), P(("wide", "narrow"), None)),
        check_vma=False,
    )
```

```python
import functools

import jax
import jax.numpy as jnp
from jax import lax
from jax.experimental import pallas as pl
from jax.experimental.pallas import tpu as pltpu
from jax.sharding import PartitionSpec as P

STEPS = 4
SIDES = 2
PLACES = 16
SMEM = pl.BlockSpec(memory_space=pltpu.SMEM)
VMEM = pl.BlockSpec(memory_space=pltpu.VMEM)
ANY = pl.BlockSpec(memory_space=pl.ANY)
HBM = pl.BlockSpec(memory_space=pltpu.HBM)


def params(mebibytes):
    return pltpu.CompilerParams(vmem_limit_bytes=mebibytes * 1024 * 1024)


def normalized_rows(value_entries):
    wide_vals = value_entries.astype(jnp.float32)
    inverse = lax.rsqrt(jnp.sum(wide_vals * wide_vals, axis=-1, keepdims=True) + 1e-06)
    return (wide_vals * inverse).astype(jnp.bfloat16)


def copies_kernel(value_ref, out_ref, sent):
    stores = [
        pltpu.make_async_copy(value_ref, out_ref.at[i], sent.at[i])
        for i in range(out_ref.shape[0])
    ]
    for store in stores:
        store.start()
    for store in stores:
        store.wait()


def copies_call(value, receivers):
    return pl.pallas_call(
        copies_kernel,
        in_specs=[VMEM],
        out_specs=HBM,
        out_shape=pltpu.HBM((receivers, *value.shape), value.dtype),
        scratch_shapes=[pltpu.SemaphoreType.DMA((receivers,))],
        compiler_params=params(8),
    )(value)


def text_kernel(*refs):
    *text_refs, unit_ref = refs
    rows = text_refs[0].shape[0]
    for i, ref in enumerate(text_refs):
        unit_ref[i * rows : (i + 1) * rows, :] = normalized_rows(ref[...])


def text_call(texts, later):
    rows, width = texts[0].shape
    return pl.pallas_call(
        text_kernel,
        in_specs=[VMEM] * len(texts),
        out_specs=VMEM,
        out_shape=jax.ShapeDtypeStruct((len(texts) * rows, width), jnp.bfloat16),
        cost_estimate=pl.CostEstimate(flops=later, bytes_accessed=10**6, transcendentals=0),
        compiler_params=params(8),
    )(*texts)


def sum_kernel(*refs):
    *value_refs, out_ref = refs
    total = value_refs[0][...].astype(jnp.float32)
    for ref in value_refs[1:]:
        total += ref[...].astype(jnp.float32)
    out_ref[...] = total.astype(out_ref.dtype)


def sum_call(values, kind, later):
    return pl.pallas_call(
        sum_kernel,
        in_specs=[VMEM] * len(values),
        out_specs=VMEM,
        out_shape=jax.ShapeDtypeStruct(values[0].shape, kind),
        cost_estimate=pl.CostEstimate(flops=later, bytes_accessed=10**6, transcendentals=0),
        compiler_params=params(8),
    )(*values)


def sides_kernel(pieces_ref, near_ref, far_ref):
    for side, ref in enumerate((near_ref, far_ref)):
        total = pieces_ref[0, side].astype(jnp.float32)
        for sender in range(1, pieces_ref.shape[0]):
            total += pieces_ref[sender, side].astype(jnp.float32)
        ref[...] = total.astype(ref.dtype)


def sides_call(pieces):
    block = pieces.shape[2:]
    return pl.pallas_call(
        sides_kernel,
        in_specs=[VMEM],
        out_specs=[VMEM] * SIDES,
        out_shape=[
            jax.ShapeDtypeStruct(block, jnp.float32),
            jax.ShapeDtypeStruct(block, jnp.bfloat16),
        ],
        compiler_params=params(8),
    )(pieces)


def join_texts(near_ref, moved_ref, text):
    rows = near_ref.shape[0] // 2
    text[:rows, :] = near_ref[:rows, :]
    text[rows : 2 * rows, :] = near_ref[rows:, :] + moved_ref[2 * rows :, :]
    text[2 * rows :, :] = moved_ref[: 2 * rows, :]


def chances(scale, shift, text, image):
    score = lax.dot_general(
        image[...], text[...], (((1,), (1,)), ((), ())), preferred_element_type=jnp.float32
    )
    return 1.0 / (1.0 + jnp.exp(-(scale * score + shift)))


def send_partial(coef, text, held, out_ref, sems, side):
    rows = held.shape[2]
    stores = []
    for i in range(held.shape[0]):
        block = jnp.dot(
            coef[i * rows : (i + 1) * rows, :], text[...], preferred_element_type=jnp.float32
        )
        held[i, side] = block.astype(jnp.bfloat16)
        store = pltpu.make_async_copy(held.at[i, side], out_ref.at[i, side], sems.at[i, side])
        store.start()
        stores.append(store)
    return stores


def pair_kernel(
    scale_ref, shift_ref, place_ref, label_ref, near_ref, moved_ref, near_image_ref, far_image_ref,
    partial_ref, own_ref, crossed_ref, kept_ref, other_ref,
    text, near, far, sent, grads, halves, stored, grad_stored,
):
    rows = near_ref.shape[0] // 2
    join_texts(near_ref, moved_ref, text)
    near[...] = normalized_rows(near_image_ref[...])
    scale, shift = scale_ref[0], shift_ref[0]
    chance = chances(scale, shift, text, near)
    far[...] = normalized_rows(far_image_ref[...])
    index = lax.broadcasted_iota(jnp.int32, (near.shape[0], rows), 0)
    image_row = (index // rows) * (SIDES * rows) + index % rows + place_ref[0]
    matched = jnp.where(label_ref[...] == image_row, 1.0, 0.0)
    chance = jnp.concatenate([chance[:, :rows] - matched, chance[:, rows:]], axis=1)
    near_coef = (scale * chance).astype(jnp.bfloat16)
    far_coef = (scale * chances(scale, shift, text, far)).astype(jnp.bfloat16)
    stores = send_partial(near_coef, text, sent, partial_ref, stored, 0)
    stores += send_partial(far_coef, text, sent, partial_ref, stored, 1)
    over_images = (((0,), (0,)), ((), ()))
    grad = lax.dot_general(near_coef, near[...], over_images, preferred_element_type=jnp.float32)
    grad += lax.dot_general(far_coef, far[...], over_images, preferred_element_type=jnp.float32)
    for i, ref in enumerate((own_ref, crossed_ref, kept_ref, other_ref)):
        place = (halves if ref.dtype == jnp.bfloat16 else grads).at[i // 2]
        place[...] = grad[i * rows : (i + 1) * rows].astype(ref.dtype)
        store = pltpu.make_async_copy(place, ref, grad_stored.at[i])
        store.start()
        stores.append(store)
    for store in stores:
        store.wait()


def pair_call(scale, shift, place, labels, texts, near, far):
    count, width = near.shape
    rows = texts[0].shape[0] // 2
    blocks = (count // rows, SIDES, rows, width)
    types = (jnp.float32, jnp.bfloat16, jnp.float32, jnp.bfloat16)
    return pl.pallas_call(
        pair_kernel,
        in_specs=[SMEM] * 3 + [VMEM] * 5,
        out_specs=[HBM] * 5,
        out_shape=[pltpu.HBM(blocks, jnp.bfloat16)]
        + [pltpu.HBM((rows, width), kind) for kind in types],
        scratch_shapes=[
            pltpu.VMEM((STEPS * rows, width), jnp.bfloat16),
            pltpu.VMEM((count, width), jnp.bfloat16),
            pltpu.VMEM((count, width), jnp.bfloat16),
            pltpu.VMEM(blocks, jnp.bfloat16),
            pltpu.VMEM((2, rows, width), jnp.float32),
            pltpu.VMEM((2, rows, width), jnp.bfloat16),
            pltpu.SemaphoreType.DMA(blocks[:2]),
            pltpu.SemaphoreType.DMA((len(types),)),
        ],
        compiler_params=params(20),
    )(scale, shift, place, labels, *texts, near, far)


def local(
    caption_vectors, picture_vectors, matching_picture_index, sharpness_multiplier, offset_shift
):
    rows, width = caption_vectors.shape
    wide, narrow = lax.axis_size("wide"), lax.axis_size("narrow")
    over_x = [[SIDES * x + y for x in range(narrow // SIDES)] for y in range(SIDES)]

    def along_wide(value, even, odd, sends=lambda w: True):
        pairs = [(w, (w + (odd if w % 2 else even)) % wide) for w in range(wide) if sends(w)]
        return lax.ppermute(value, "wide", pairs)

    def last(w):
        return w % PLACES >= PLACES - 2

    def first(w):
        return w % PLACES < 2

    def twin(value):
        return along_wide(value, 1, -1)

    def across(value):
        return lax.ppermute(value, "narrow", [(n, n ^ 1) for n in range(narrow)])

    def exchange(value):
        return lax.all_to_all(
            value, "narrow", split_axis=0, concat_axis=0, tiled=True, axis_index_groups=over_x
        )

    def spread(value):
        return exchange(copies_call(value, narrow // SIDES)).reshape(-1, width)

    swapped = across(picture_vectors)
    detour = along_wide(caption_vectors, -4, -4, lambda w: w % 2 and last(w))
    mine = along_wide(caption_vectors, 2, 2, lambda w: w % 2 == 0 or not last(w))
    mine += along_wide(detour, 6, 6, lambda w: w % PLACES == PLACES - 5)
    cross = along_wide(caption_vectors, 1, 3, lambda w: w % 2 == 0 or not last(w))
    passed = along_wide(mine, 1, 1, lambda w: w % 2 and first(w))
    near = spread(picture_vectors)
    swapped, near = lax.optimization_barrier((swapped, near))
    far = spread(swapped)
    texts = [text_call([caption_vectors, cross], 6000000000), text_call([mine, twin(mine), passed], 1000000000)]

    scale, shift = sharpness_multiplier[None], offset_shift[None]
    place = lax.axis_index("wide") * (rows * narrow) + (lax.axis_index("narrow") % SIDES) * rows
    place = place.astype(jnp.int32)[None]
    partial_value, own, crossed, kept, other = pair_call(
        scale, shift, place, matching_picture_index[None, :], texts, near, far
    )
    near_sum, far_sum = sides_call(exchange(partial_value))
    image_grad = near_sum + across(far_sum).astype(jnp.float32)
    detoured = along_wide(crossed, 3, 3, lambda w: w % 2 == 0 and first(w))
    detoured = along_wide(detoured, -6, -6, lambda w: w % PLACES == 3)
    crossed = along_wide(crossed, -3, -1, lambda w: w % 2 or not first(w))
    kept = along_wide((kept + twin(other).astype(jnp.float32)).astype(jnp.bfloat16), -2, -2)
    text_grad = sum_call([own, kept, crossed, detoured], jnp.bfloat16, 10**6)
    return (text_grad, image_grad.astype(jnp.bfloat16))


def solution(mesh):
    placed = (
        P(("wide", "narrow"), None),
        P(("wide", "narrow"), None),
        P(("wide", "narrow")),
        P(),
        P(),
    )
    return jax.shard_map(
        local,
        mesh=mesh,
        in_specs=placed,
        out_specs=(P(("wide", "narrow"), None), P(("wide", "narrow"), None)),
        check_vma=False,
    )
```

```python
import functools

import jax
import jax.numpy as jnp
from jax import lax
from jax.experimental import pallas as pl
from jax.experimental.pallas import tpu as pltpu
from jax.sharding import PartitionSpec as P

STEPS = 4
SIDES = 2
PLACES = 16
SMEM = pl.BlockSpec(memory_space=pltpu.SMEM)
VMEM = pl.BlockSpec(memory_space=pltpu.VMEM)
ANY = pl.BlockSpec(memory_space=pl.ANY)
HBM = pl.BlockSpec(memory_space=pltpu.HBM)


def params(mebibytes):
    return pltpu.CompilerParams(vmem_limit_bytes=mebibytes * 1024 * 1024)


def normalized_rows(value_entries):
    wide_vals = value_entries.astype(jnp.float32)
    inverse = lax.rsqrt(jnp.sum(wide_vals * wide_vals, axis=-1, keepdims=True) + 1e-06)
    return (wide_vals * inverse).astype(jnp.bfloat16)


def copies_kernel(value_ref, out_ref, sent):
    stores = [
        pltpu.make_async_copy(value_ref, out_ref.at[i], sent.at[i])
        for i in range(out_ref.shape[0])
    ]
    for store in stores:
        store.start()
    for store in stores:
        store.wait()


def copies_call(value, receivers):
    return pl.pallas_call(
        copies_kernel,
        in_specs=[VMEM],
        out_specs=HBM,
        out_shape=pltpu.HBM((receivers, *value.shape), value.dtype),
        scratch_shapes=[pltpu.SemaphoreType.DMA((receivers,))],
        compiler_params=params(8),
    )(value)


def here_kernel(own_ref, cross_ref, unit_ref):
    rows = own_ref.shape[0]
    unit_ref[:rows, :] = normalized_rows(own_ref[...])
    unit_ref[rows:, :] = normalized_rows(cross_ref[...])


def text_kernel(here_ref, mine_ref, twin_ref, passed_ref, unit_ref):
    rows = mine_ref.shape[0]
    unit_ref[: 2 * rows, :] = here_ref[...]
    unit_ref[rows : 2 * rows, :] += normalized_rows(passed_ref[...])
    unit_ref[2 * rows : 3 * rows, :] = normalized_rows(mine_ref[...])
    unit_ref[3 * rows :, :] = normalized_rows(twin_ref[...])


def text_call(kernel, operands, blocks, later):
    rows, width = operands[-1].shape
    return pl.pallas_call(
        kernel,
        in_specs=[VMEM] * len(operands),
        out_specs=VMEM,
        out_shape=jax.ShapeDtypeStruct((blocks * rows, width), jnp.bfloat16),
        cost_estimate=pl.CostEstimate(flops=later, bytes_accessed=10**6, transcendentals=0),
        compiler_params=params(8),
    )(*operands)


def sum_kernel(*refs):
    *value_refs, out_ref = refs
    total = value_refs[0][...].astype(jnp.float32)
    for ref in value_refs[1:]:
        total += ref[...].astype(jnp.float32)
    out_ref[...] = total.astype(out_ref.dtype)


def sum_call(values, kind, later):
    return pl.pallas_call(
        sum_kernel,
        in_specs=[VMEM] * len(values),
        out_specs=VMEM,
        out_shape=jax.ShapeDtypeStruct(values[0].shape, kind),
        cost_estimate=pl.CostEstimate(flops=later, bytes_accessed=10**6, transcendentals=0),
        compiler_params=params(8),
    )(*values)


def sides_kernel(pieces_ref, near_ref, far_ref):
    for side, ref in enumerate((near_ref, far_ref)):
        total = pieces_ref[0, side].astype(jnp.float32)
        for sender in range(1, pieces_ref.shape[0]):
            total += pieces_ref[sender, side].astype(jnp.float32)
        ref[...] = total.astype(ref.dtype)


def sides_call(pieces):
    block = pieces.shape[2:]
    return pl.pallas_call(
        sides_kernel,
        in_specs=[VMEM],
        out_specs=[VMEM] * SIDES,
        out_shape=[
            jax.ShapeDtypeStruct(block, jnp.float32),
            jax.ShapeDtypeStruct(block, jnp.bfloat16),
        ],
        compiler_params=params(8),
    )(pieces)


def chances(scale, shift, text, image):
    score = lax.dot_general(
        image[...], text[...], (((1,), (1,)), ((), ())), preferred_element_type=jnp.float32
    )
    return 1.0 / (1.0 + jnp.exp(-(scale * score + shift)))


def send_partial(coef, text, held, out_ref, sems, side):
    rows = held.shape[2]
    stores = []
    for i in range(held.shape[0]):
        block = jnp.dot(
            coef[i * rows : (i + 1) * rows, :], text[...], preferred_element_type=jnp.float32
        )
        held[i, side] = block.astype(jnp.bfloat16)
        store = pltpu.make_async_copy(held.at[i, side], out_ref.at[i, side], sems.at[i, side])
        store.start()
        stores.append(store)
    return stores


def pair_kernel(
    scale_ref, shift_ref, place_ref, label_ref, text, near_image_ref, far_image_ref,
    partial_ref, own_ref, crossed_ref, kept_ref, other_ref,
    near, far, sent, grads, halves, stored, grad_stored,
):
    rows = text.shape[0] // STEPS
    near[...] = normalized_rows(near_image_ref[...])
    scale, shift = scale_ref[0], shift_ref[0]
    chance = chances(scale, shift, text, near)
    far[...] = normalized_rows(far_image_ref[...])
    index = lax.broadcasted_iota(jnp.int32, (near.shape[0], rows), 0)
    image_row = (index // rows) * (SIDES * rows) + index % rows + place_ref[0]
    matched = jnp.where(label_ref[...] == image_row, 1.0, 0.0)
    chance = jnp.concatenate([chance[:, :rows] - matched, chance[:, rows:]], axis=1)
    near_coef = (scale * chance).astype(jnp.bfloat16)
    far_coef = (scale * chances(scale, shift, text, far)).astype(jnp.bfloat16)
    stores = send_partial(near_coef, text, sent, partial_ref, stored, 0)
    stores += send_partial(far_coef, text, sent, partial_ref, stored, 1)
    over_images = (((0,), (0,)), ((), ()))
    grad = lax.dot_general(near_coef, near[...], over_images, preferred_element_type=jnp.float32)
    grad += lax.dot_general(far_coef, far[...], over_images, preferred_element_type=jnp.float32)
    for i, ref in enumerate((own_ref, crossed_ref, kept_ref, other_ref)):
        place = (halves if ref.dtype == jnp.bfloat16 else grads).at[i // 2]
        place[...] = grad[i * rows : (i + 1) * rows].astype(ref.dtype)
        store = pltpu.make_async_copy(place, ref, grad_stored.at[i])
        store.start()
        stores.append(store)
    for store in stores:
        store.wait()


def pair_call(scale, shift, place, labels, text, near, far):
    count, width = near.shape
    rows = text.shape[0] // STEPS
    blocks = (count // rows, SIDES, rows, width)
    types = (jnp.float32, jnp.bfloat16, jnp.float32, jnp.bfloat16)
    return pl.pallas_call(
        pair_kernel,
        in_specs=[SMEM] * 3 + [VMEM] * 4,
        out_specs=[HBM] * 5,
        out_shape=[pltpu.HBM(blocks, jnp.bfloat16)]
        + [pltpu.HBM((rows, width), kind) for kind in types],
        scratch_shapes=[
            pltpu.VMEM((count, width), jnp.bfloat16),
            pltpu.VMEM((count, width), jnp.bfloat16),
            pltpu.VMEM(blocks, jnp.bfloat16),
            pltpu.VMEM((2, rows, width), jnp.float32),
            pltpu.VMEM((2, rows, width), jnp.bfloat16),
            pltpu.SemaphoreType.DMA(blocks[:2]),
            pltpu.SemaphoreType.DMA((len(types),)),
        ],
        compiler_params=params(20),
    )(scale, shift, place, labels, text, near, far)


def local(
    caption_vectors, picture_vectors, matching_picture_index, sharpness_multiplier, offset_shift
):
    rows, width = caption_vectors.shape
    wide, narrow = lax.axis_size("wide"), lax.axis_size("narrow")
    over_x = [[SIDES * x + y for x in range(narrow // SIDES)] for y in range(SIDES)]

    def along_wide(value, even, odd, sends=lambda w: True):
        pairs = [(w, (w + (odd if w % 2 else even)) % wide) for w in range(wide) if sends(w)]
        return lax.ppermute(value, "wide", pairs)

    def last(w):
        return w % PLACES >= PLACES - 2

    def first(w):
        return w % PLACES < 2

    def twin(value):
        return along_wide(value, 1, -1)

    def across(value):
        return lax.ppermute(value, "narrow", [(n, n ^ 1) for n in range(narrow)])

    def exchange(value):
        return lax.all_to_all(
            value, "narrow", split_axis=0, concat_axis=0, tiled=True, axis_index_groups=over_x
        )

    def spread(value):
        return exchange(copies_call(value, narrow // SIDES)).reshape(-1, width)

    swapped = across(picture_vectors)
    detour = along_wide(caption_vectors, -4, -4, lambda w: w % 2 and last(w))
    mine = along_wide(caption_vectors, 2, 2, lambda w: w % 2 == 0 or not last(w))
    mine += along_wide(detour, 6, 6, lambda w: w % PLACES == PLACES - 5)
    cross = along_wide(caption_vectors, 1, 3, lambda w: w % 2 == 0 or not last(w))
    passed = along_wide(mine, 1, 1, lambda w: w % 2 and first(w))
    near = spread(picture_vectors)
    swapped, near = lax.optimization_barrier((swapped, near))
    far = spread(swapped)
    here = text_call(here_kernel, [caption_vectors, cross], 2, 6000000000)
    text = text_call(text_kernel, [here, mine, twin(mine), passed], STEPS, 1000000000)

    scale, shift = sharpness_multiplier[None], offset_shift[None]
    place = lax.axis_index("wide") * (rows * narrow) + (lax.axis_index("narrow") % SIDES) * rows
    place = place.astype(jnp.int32)[None]
    partial_value, own, crossed, kept, other = pair_call(
        scale, shift, place, matching_picture_index[None, :], text, near, far
    )
    near_sum, far_sum = sides_call(exchange(partial_value))
    image_grad = near_sum + across(far_sum).astype(jnp.float32)
    detoured = along_wide(crossed, 3, 3, lambda w: w % 2 == 0 and first(w))
    detoured = along_wide(detoured, -6, -6, lambda w: w % PLACES == 3)
    crossed = along_wide(crossed, -3, -1, lambda w: w % 2 or not first(w))
    kept = along_wide((kept + twin(other).astype(jnp.float32)).astype(jnp.bfloat16), -2, -2)
    text_grad = sum_call([own, kept, crossed, detoured], jnp.bfloat16, 10**6)
    return (text_grad, image_grad.astype(jnp.bfloat16))


def solution(mesh):
    placed = (
        P(("wide", "narrow"), None),
        P(("wide", "narrow"), None),
        P(("wide", "narrow")),
        P(),
        P(),
    )
    return jax.shard_map(
        local,
        mesh=mesh,
        in_specs=placed,
        out_specs=(P(("wide", "narrow"), None), P(("wide", "narrow"), None)),
        check_vma=False,
    )
```

```python
import functools

import jax
import jax.numpy as jnp
from jax import lax
from jax.experimental import pallas as pl
from jax.experimental.pallas import tpu as pltpu
from jax.sharding import PartitionSpec as P

STEPS = 4
SIDES = 2
PLACES = 16
SMEM = pl.BlockSpec(memory_space=pltpu.SMEM)
VMEM = pl.BlockSpec(memory_space=pltpu.VMEM)
ANY = pl.BlockSpec(memory_space=pl.ANY)
HBM = pl.BlockSpec(memory_space=pltpu.HBM)


def params(mebibytes):
    return pltpu.CompilerParams(vmem_limit_bytes=mebibytes * 1024 * 1024)


def normalized_rows(value_entries):
    wide_vals = value_entries.astype(jnp.float32)
    inverse = lax.rsqrt(jnp.sum(wide_vals * wide_vals, axis=-1, keepdims=True) + 1e-06)
    return (wide_vals * inverse).astype(jnp.bfloat16)


def copies_kernel(value_ref, out_ref, sent):
    stores = [
        pltpu.make_async_copy(value_ref, out_ref.at[i], sent.at[i])
        for i in range(out_ref.shape[0])
    ]
    for store in stores:
        store.start()
    for store in stores:
        store.wait()


def copies_call(value, receivers):
    return pl.pallas_call(
        copies_kernel,
        in_specs=[VMEM],
        out_specs=HBM,
        out_shape=pltpu.HBM((receivers, *value.shape), value.dtype),
        scratch_shapes=[pltpu.SemaphoreType.DMA((receivers,))],
        compiler_params=params(8),
    )(value)


def here_kernel(own_ref, cross_ref, unit_ref):
    rows = own_ref.shape[0]
    unit_ref[:rows, :] = normalized_rows(own_ref[...])
    unit_ref[rows:, :] = normalized_rows(cross_ref[...])


def text_kernel(here_ref, mine_ref, twin_ref, passed_ref, unit_ref):
    rows = mine_ref.shape[0]
    unit_ref[: 2 * rows, :] = here_ref[...]
    unit_ref[rows : 2 * rows, :] += normalized_rows(passed_ref[...])
    unit_ref[2 * rows : 3 * rows, :] = normalized_rows(mine_ref[...])
    unit_ref[3 * rows :, :] = normalized_rows(twin_ref[...])


def text_call(kernel, operands, blocks, later):
    rows, width = operands[-1].shape
    return pl.pallas_call(
        kernel,
        in_specs=[VMEM] * len(operands),
        out_specs=VMEM,
        out_shape=jax.ShapeDtypeStruct((blocks * rows, width), jnp.bfloat16),
        cost_estimate=pl.CostEstimate(flops=later, bytes_accessed=10**6, transcendentals=0),
        compiler_params=params(8),
    )(*operands)


def sum_kernel(*refs):
    *value_refs, out_ref = refs
    total = value_refs[0][...].astype(jnp.float32)
    for ref in value_refs[1:]:
        total += ref[...].astype(jnp.float32)
    out_ref[...] = total.astype(out_ref.dtype)


def sum_call(values, kind, later):
    return pl.pallas_call(
        sum_kernel,
        in_specs=[VMEM] * len(values),
        out_specs=VMEM,
        out_shape=jax.ShapeDtypeStruct(values[0].shape, kind),
        cost_estimate=pl.CostEstimate(flops=later, bytes_accessed=10**6, transcendentals=0),
        compiler_params=params(8),
    )(*values)


def sides_kernel(pieces_ref, near_ref, far_ref):
    for side, ref in enumerate((near_ref, far_ref)):
        total = pieces_ref[0, side].astype(jnp.float32)
        for sender in range(1, pieces_ref.shape[0]):
            total += pieces_ref[sender, side].astype(jnp.float32)
        ref[...] = total.astype(ref.dtype)


def sides_call(pieces):
    block = pieces.shape[2:]
    return pl.pallas_call(
        sides_kernel,
        in_specs=[VMEM],
        out_specs=[VMEM] * SIDES,
        out_shape=[
            jax.ShapeDtypeStruct(block, jnp.float32),
            jax.ShapeDtypeStruct(block, jnp.bfloat16),
        ],
        compiler_params=params(8),
    )(pieces)


def chances(scale, shift, text, image):
    score = lax.dot_general(
        image[...], text[...], (((1,), (1,)), ((), ())), preferred_element_type=jnp.float32
    )
    return 1.0 / (1.0 + jnp.exp(-(scale * score + shift)))


def send_partial(coef, text, held, out_ref, sems, side):
    rows = held.shape[2]
    stores = []
    for i in range(held.shape[0]):
        block = jnp.dot(
            coef[i * rows : (i + 1) * rows, :], text[...], preferred_element_type=jnp.float32
        )
        held[i, side] = block.astype(jnp.bfloat16)
        store = pltpu.make_async_copy(held.at[i, side], out_ref.at[i, side], sems.at[i, side])
        store.start()
        stores.append(store)
    return stores


def pair_kernel(
    scale_ref, shift_ref, place_ref, label_ref, text, near_image_ref, far_image_ref,
    partial_ref, own_ref, crossed_ref, kept_ref, other_ref,
    near, far, sent, grads, halves, stored, grad_stored,
):
    rows = text.shape[0] // STEPS
    near[...] = normalized_rows(near_image_ref[...])
    scale, shift = scale_ref[0], shift_ref[0]
    chance = chances(scale, shift, text, near)
    far[...] = normalized_rows(far_image_ref[...])
    index = lax.broadcasted_iota(jnp.int32, (near.shape[0], rows), 0)
    image_row = (index // rows) * (SIDES * rows) + index % rows + place_ref[0]
    matched = jnp.where(label_ref[...] == image_row, 1.0, 0.0)
    chance = jnp.concatenate([chance[:, :rows] - matched, chance[:, rows:]], axis=1)
    near_coef = (scale * chance).astype(jnp.bfloat16)
    far_coef = (scale * chances(scale, shift, text, far)).astype(jnp.bfloat16)
    stores = send_partial(near_coef, text, sent, partial_ref, stored, 0)
    stores += send_partial(far_coef, text, sent, partial_ref, stored, 1)
    over_images = (((0,), (0,)), ((), ()))
    grad = lax.dot_general(near_coef, near[...], over_images, preferred_element_type=jnp.float32)
    grad += lax.dot_general(far_coef, far[...], over_images, preferred_element_type=jnp.float32)
    for i, ref in enumerate((own_ref, crossed_ref, kept_ref, other_ref)):
        place = (halves if ref.dtype == jnp.bfloat16 else grads).at[i // 2]
        place[...] = grad[i * rows : (i + 1) * rows].astype(ref.dtype)
        store = pltpu.make_async_copy(place, ref, grad_stored.at[i])
        store.start()
        stores.append(store)
    for store in stores:
        store.wait()


def pair_call(scale, shift, place, labels, text, near, far):
    count, width = near.shape
    rows = text.shape[0] // STEPS
    blocks = (count // rows, SIDES, rows, width)
    types = (jnp.float32, jnp.bfloat16, jnp.float32, jnp.bfloat16)
    return pl.pallas_call(
        pair_kernel,
        in_specs=[SMEM] * 3 + [VMEM] * 4,
        out_specs=[HBM] * 5,
        out_shape=[pltpu.HBM(blocks, jnp.bfloat16)]
        + [pltpu.HBM((rows, width), kind) for kind in types],
        scratch_shapes=[
            pltpu.VMEM((count, width), jnp.bfloat16),
            pltpu.VMEM((count, width), jnp.bfloat16),
            pltpu.VMEM(blocks, jnp.bfloat16),
            pltpu.VMEM((2, rows, width), jnp.float32),
            pltpu.VMEM((2, rows, width), jnp.bfloat16),
            pltpu.SemaphoreType.DMA(blocks[:2]),
            pltpu.SemaphoreType.DMA((len(types),)),
        ],
        compiler_params=params(20),
    )(scale, shift, place, labels, text, near, far)


def local(
    caption_vectors, picture_vectors, matching_picture_index, sharpness_multiplier, offset_shift
):
    rows, width = caption_vectors.shape
    wide, narrow = lax.axis_size("wide"), lax.axis_size("narrow")
    over_x = [[SIDES * x + y for x in range(narrow // SIDES)] for y in range(SIDES)]

    def along_wide(value, even, odd, sends=lambda w: True):
        pairs = [(w, (w + (odd if w % 2 else even)) % wide) for w in range(wide) if sends(w)]
        return lax.ppermute(value, "wide", pairs)

    def last(w):
        return w % PLACES >= PLACES - 2

    def first(w):
        return w % PLACES < 2

    def twin(value):
        return along_wide(value, 1, -1)

    def across(value):
        return lax.ppermute(value, "narrow", [(n, n ^ 1) for n in range(narrow)])

    def exchange(value):
        return lax.all_to_all(
            value, "narrow", split_axis=0, concat_axis=0, tiled=True, axis_index_groups=over_x
        )

    def spread(value):
        return exchange(copies_call(value, narrow // SIDES)).reshape(-1, width)

    swapped = across(picture_vectors)
    mine = along_wide(caption_vectors, 2, 2)
    cross = along_wide(caption_vectors, 1, 3, lambda w: w % 2 == 0 or not last(w))
    passed = along_wide(mine, 1, 1, lambda w: w % 2 and first(w))
    near = spread(picture_vectors)
    swapped, near = lax.optimization_barrier((swapped, near))
    far = spread(swapped)
    here = text_call(here_kernel, [caption_vectors, cross], 2, 6000000000)
    text = text_call(text_kernel, [here, mine, twin(mine), passed], STEPS, 1000000000)

    scale, shift = sharpness_multiplier[None], offset_shift[None]
    place = lax.axis_index("wide") * (rows * narrow) + (lax.axis_index("narrow") % SIDES) * rows
    place = place.astype(jnp.int32)[None]
    partial_value, own, crossed, kept, other = pair_call(
        scale, shift, place, matching_picture_index[None, :], text, near, far
    )
    near_sum, far_sum = sides_call(exchange(partial_value))
    image_grad = near_sum + across(far_sum).astype(jnp.float32)
    detoured = along_wide(crossed, 3, 3, lambda w: w % 2 == 0 and first(w))
    detoured = along_wide(detoured, -6, -6, lambda w: w % PLACES == 3)
    crossed = along_wide(crossed, -3, -1, lambda w: w % 2 or not first(w))
    kept = along_wide((kept + twin(other).astype(jnp.float32)).astype(jnp.bfloat16), -2, -2)
    text_grad = sum_call([own, kept, crossed, detoured], jnp.bfloat16, 10**6)
    return (text_grad, image_grad.astype(jnp.bfloat16))


def solution(mesh):
    placed = (
        P(("wide", "narrow"), None),
        P(("wide", "narrow"), None),
        P(("wide", "narrow")),
        P(),
        P(),
    )
    return jax.shard_map(
        local,
        mesh=mesh,
        in_specs=placed,
        out_specs=(P(("wide", "narrow"), None), P(("wide", "narrow"), None)),
        check_vma=False,
    )
```
